32 devices in a mesh: groups: 2 (over y), site: 4 (over z), rep: 4 (over x, core).
Axes of the slice: x: 2, y: 2, z: 4, core: 2. Of those that a mesh axis runs over, the one named last changes fastest.
Arguments:
- features: bfloat16 [16, 65536], P(None, ('groups', 'site')), parts along dimension 1, may hold values from -6 to 6
- inverse_scale: float32 [32], P('groups'), parts along dimension 0, may hold values from 0.05 to 0.15
- right_sides: bfloat16 [16, 65536], P(None, ('groups', 'site')), parts along dimension 1, may hold values from -0.3984375 to 0.3984375
- block_order: int32 [8, 8192], P(('groups', 'site')), parts along dimension 0, may hold values from 0 to 8191, each once within a row
- block_pairs: int32 [8, 4, 2, 32], P(('groups', 'site'), 'rep'), parts along dimension 0, may hold values from 0 to 63, as said below
- pair_count: int32 [8, 4], P(('groups', 'site'), 'rep'), parts along dimension 0, may hold values from 1 to 32, as said below
Outputs:
- product: float32 [16, 65536], P('rep', ('groups', 'site')), parts along dimension 1
The draws below stay inside these ranges and needn't reach their ends.
There are 2 independent parts, one for each index of `groups`. The reference program is written for one: setup_inputs(seed, part) draws one part's arguments, and reference() takes and returns one part's arrays. A program takes and returns all parts, laid end to end along the dimension named above; each array names one. Nothing has to cross between parts.
Inputs may be any that keep to these rules, and one draw needn't show every extreme that they name: `block_pairs`: for the device at site s, each slot holds two different blocks: the first one of the lower half of site s's blocks (s * 16 to s * 16 + 16 // 2 - 1), the second one of the upper half of some site's blocks. Among a device's counted slots at most 8 have their second block at one site, and some device reaches 8 in every draw. Each unordered pair of blocks stands in at most one counted slot of all devices. Slots from pair_count on are ignored. `pair_count`: some device has all 32 slots counted in every draw. `block_order`: each row is a permutation.
All inputs are finite; a program needn't handle non-finite values.
Results may differ from the reference program's by a relative error of at most 0.0031.
Values may be sent and summed in bfloat16 or wider, within the bound.
A program may use at most 64 MiB of HBM per device.

```python
import math
import jax
import jax.numpy as jnp
from jax import lax

FEATURE_DIM = 16
SIDES = 16
BLOCK_LEN = 512
SITE_BLOCKS = 16
PAIR_SLOTS = 32
SITE_COUNT = 4
REP_COUNT = 4
SLOT_CAP = 8
SITE_RECORDS = 8192
ALL_BLOCKS = 64
ALL_RECORDS = 32768


def draw_block_pairs(key, part):
    key = jax.random.fold_in(key, 11)
    half_blocks = SITE_BLOCKS // 2
    code_span = half_blocks * half_blocks
    home_keys = jax.random.split(jax.random.fold_in(key, 1), SITE_COUNT * REP_COUNT)
    home_order = jax.vmap(lambda subkey: jax.random.permutation(subkey, SITE_COUNT))(home_keys)
    home_order = home_order.reshape(SITE_COUNT, REP_COUNT, SITE_COUNT).astype(jnp.int32)
    slot_ids = jnp.arange(PAIR_SLOTS, dtype=jnp.int32)
    home_sites = jnp.take(home_order, slot_ids % SITE_COUNT, axis=2)
    repeat_ids = slot_ids // SITE_COUNT
    code_keys = jax.random.split(jax.random.fold_in(key, 2), SITE_COUNT * SITE_COUNT)
    codes = jax.vmap(lambda subkey: jax.random.permutation(subkey, code_span))(code_keys).reshape(-1).astype(jnp.int32)
    site_ids = jnp.arange(SITE_COUNT, dtype=jnp.int32)[:, None, None]
    rep_ids = jnp.arange(REP_COUNT, dtype=jnp.int32)[None, :, None]
    code_pos = (site_ids * SITE_COUNT + home_sites) * code_span + rep_ids * SLOT_CAP + repeat_ids[None, None, :]
    picked = jnp.take(codes, code_pos.astype(jnp.int32), axis=0)
    lower_ids = picked // half_blocks
    upper_ids = half_blocks + picked % half_blocks
    near_ids = site_ids * SITE_BLOCKS + lower_ids
    far_ids = home_sites * SITE_BLOCKS + upper_ids
    return jnp.stack([near_ids, far_ids], axis=2).astype(jnp.int32)


def draw_pair_count(key, part):
    key = jax.random.fold_in(key, 23)
    counts = jax.random.randint(jax.random.fold_in(key, 1), (SITE_COUNT, REP_COUNT), 1, PAIR_SLOTS + 1)
    busiest = jax.random.randint(jax.random.fold_in(key, 2), (), 0, SITE_COUNT * REP_COUNT)
    device_ids = jnp.arange(SITE_COUNT * REP_COUNT, dtype=jnp.int32).reshape(SITE_COUNT, REP_COUNT)
    return jnp.where(device_ids == busiest, PAIR_SLOTS, counts).astype(jnp.int32)


def levels(key, shape, pieces, smallest, largest):
    def one(position, blocks):
        draws = jax.random.uniform(jax.random.fold_in(jax.random.fold_in(key, 6), position), (blocks,), jnp.float32, smallest / len(pieces), largest / len(pieces))
        return jnp.repeat(jnp.exp(draws), shape[position] // blocks).reshape((-1,) + (1,) * (len(shape) - position - 1))

    loudness = one(*pieces[0])
    for cut in pieces[1:]:
        loudness = loudness * one(*cut)
    return loudness


def normal_values(own_key, dims, deviation, reach, shards=(), held_as=jnp.bfloat16):
    values = jax.random.normal(own_key, dims, jnp.float32) * deviation
    if len(shards) > 0:
        values = levels(own_key, dims, shards, -0.22, 0.18) * values
    return jnp.clip(values, min=-reach, max=reach).astype(held_as)


def setup_inputs(seed: int = 0, part: int = 0) -> dict:
    streams_of = jax.random.split(jax.random.key(seed), 7)
    part_keys = jax.random.split(jax.random.fold_in(streams_of[6], part), 7)
    features = normal_values(part_keys[0], (FEATURE_DIM, ALL_RECORDS), 1.0, 6.0, ((1, 4),))
    inverse_scale = jnp.clip(jnp.exp(jax.random.uniform(part_keys[1], (FEATURE_DIM,), jnp.float32, math.log(0.05), math.log(0.15))), 0.05, 0.15)
    right_sides = normal_values(part_keys[2], (SIDES, ALL_RECORDS), 0.06, 0.3984375, ((1, 4),))
    block_order = jax.vmap(lambda own: jax.random.permutation(own, SITE_RECORDS))(jax.random.split(part_keys[3], SITE_COUNT)).reshape((SITE_COUNT, SITE_RECORDS)).astype(jnp.int32)
    block_pairs = draw_block_pairs(jax.random.fold_in(jax.random.fold_in(streams_of[6], part), 71), part)
    pair_count = draw_pair_count(jax.random.fold_in(jax.random.fold_in(streams_of[6], part), 71), part)
    return {"features": features, "inverse_scale": inverse_scale, "right_sides": right_sides, "block_order": block_order, "block_pairs": block_pairs, "pair_count": pair_count}


precise = lax.Precision.HIGHEST

def kernel_tile(left_raw, right_raw, inverse_scale):
    left_pts = left_raw.astype(jnp.float32) * inverse_scale[:, None]
    right_pts = right_raw.astype(jnp.float32) * inverse_scale[:, None]
    left_sq = lax.optimization_barrier(jnp.sum(left_pts * left_pts, axis=0))
    right_sq = lax.optimization_barrier(jnp.sum(right_pts * right_pts, axis=0))
    cross = lax.dot_general(left_pts, right_pts, (((0,), (0,)), ((), ())), precision=precise, preferred_element_type=jnp.float32)
    distance = jnp.sqrt(jnp.maximum(left_sq[:, None] + right_sq[None, :] - 2.0 * cross, 0.0))
    inside = jnp.maximum(1.0 - distance, 0.0)
    inside_sq = inside * inside
    return (inside_sq * inside_sq * (4.0 * distance + 1.0)).astype(jnp.bfloat16)

def toward_rows(values, weights):
    return lax.dot_general(values, weights, (((1,), (1,)), ((), ())), preferred_element_type=jnp.float32)

def toward_cols(values, weights):
    return jnp.dot(values, weights, preferred_element_type=jnp.float32)

def reference(features, inverse_scale, right_sides, block_order, block_pairs, pair_count):
    records = (block_order + (jnp.arange(SITE_COUNT, dtype=jnp.int32) * SITE_RECORDS)[:, None]).reshape(-1).astype(jnp.int32)
    block_pts = jnp.take(features, records, axis=1).reshape(FEATURE_DIM, ALL_BLOCKS, BLOCK_LEN).transpose(1, 0, 2)
    block_vals = jnp.take(right_sides, records, axis=1).reshape(SIDES, ALL_BLOCKS, BLOCK_LEN).transpose(1, 0, 2)

    def diag_step(totals, block_id):
        weights = kernel_tile(block_pts[block_id], block_pts[block_id], inverse_scale)
        return (totals.at[block_id].add(toward_rows(block_vals[block_id], weights)), None)
    start = jnp.zeros((ALL_BLOCKS, SIDES, BLOCK_LEN), jnp.float32)
    totals, _ = lax.scan(diag_step, start, jnp.arange(ALL_BLOCKS, dtype=jnp.int32))
    near_ids = block_pairs[:, :, 0].reshape(-1)
    far_ids = block_pairs[:, :, 1].reshape(-1)
    counted = (jnp.arange(PAIR_SLOTS, dtype=jnp.int32)[None, None, :] < pair_count[:, :, None]).reshape(-1)

    def pair_step(totals, item):
        near_id, far_id, active = item

        def work(current):
            weights = kernel_tile(block_pts[near_id], block_pts[far_id], inverse_scale)
            current = current.at[near_id].add(toward_rows(block_vals[far_id], weights))
            return current.at[far_id].add(toward_cols(block_vals[near_id], weights))

        def keep(current):
            return current
        return (lax.cond(active, work, keep, totals), None)
    totals, _ = lax.scan(pair_step, totals, (near_ids, far_ids, counted))
    ordered = totals.transpose(1, 0, 2).reshape(SIDES, ALL_RECORDS)
    return jnp.zeros_like(ordered).at[:, records].set(ordered)
```

```python
import functools

import jax
import jax.numpy as jnp
from jax import lax
from jax.experimental import pallas as pl
from jax.experimental.pallas import tpu as pltpu
from jax.sharding import PartitionSpec as P

BLOCK_LEN = 512
LOW = 256
DEPTH = 64
LINK = jnp.float32
F32, BF16 = jnp.float32, jnp.bfloat16
VMEM = pl.BlockSpec(memory_space=pltpu.VMEM)
SMEM = pl.BlockSpec(memory_space=pltpu.SMEM)
NT = (((1,), (1,)), ((), ()))


def rep_peer(step, reps):
    return lax.rem(lax.axis_index("rep") + step, reps)


def site_peer(step, sites):
    return lax.rem(lax.axis_index("site") + step, sites)


def collect_kernel(
    sites, reps, feat_ref, side_ref, order_ref, pairs_ref, count_ref,
    low_ref, far_ref, up_ref, all_pairs_ref, all_count_ref,
    stack, rep_send, rep_recv, site_send, site_recv,
):
    site, rep = lax.axis_index("site"), lax.axis_index("rep")
    feat_dim, site_len = feat_ref.shape
    width = feat_dim + side_ref.shape[0]
    high_total = site_len // LOW
    far_cols = far_ref.shape[3]
    half = far_ref.shape[1]
    own = low_ref.shape[1]

    barrier = pltpu.get_barrier_semaphore()
    for step in range(1, reps):
        pl.semaphore_signal(barrier, inc=1, device_id={"rep": rep_peer(step, reps)})

    @pl.loop(1, sites)
    def _(step):
        pl.semaphore_signal(barrier, inc=1, device_id={"site": site_peer(step, sites)})

    for high in range(high_total):
        cols = slice(high * LOW, (high + 1) * LOW)
        stack[high * width : high * width + feat_dim, :] = feat_ref[:, cols]
        stack[high * width + feat_dim : (high + 1) * width, :] = side_ref[:, cols]
    all_pairs_ref[rep] = pairs_ref[...]
    all_count_ref[rep] = count_ref[...]

    def pick(start):
        index = order_ref[:, start : start + LOW]
        low = index % LOW
        high_part = index // LOW
        spot = lax.broadcasted_iota(jnp.int32, (LOW, LOW), 0) == low
        spot = jnp.where(spot, 1.0, 0.0).astype(BF16)
        picked = jnp.zeros((width, LOW), F32)
        group = 8
        for first in range(0, high_total, group):
            part = jnp.dot(
                stack[first * width : (first + group) * width, :], spot,
                preferred_element_type=F32,
            )
            for inner in range(group):
                hit = jnp.broadcast_to(high_part == first + inner, (width, LOW))
                picked = jnp.where(hit, part[inner * width : (inner + 1) * width], picked)
        return picked.astype(BF16)

    per_chunk = LOW // far_cols
    for chunk in range(half // per_chunk):
        picked = pick(chunk * LOW)
        for inner in range(per_chunk):
            far_ref[site, chunk * per_chunk + inner] = picked[
                :, inner * far_cols : (inner + 1) * far_cols
            ]

    pl.semaphore_wait(barrier, reps - 1 + sites - 1)

    def site_copy(step):
        return pltpu.make_async_remote_copy(
            src_ref=far_ref.at[site], dst_ref=far_ref.at[site],
            send_sem=site_send.at[step], recv_sem=site_recv.at[step],
            device_id={"site": site_peer(step, sites)},
        )

    def rep_copies(step):
        copies = []
        for kind, ref in enumerate((all_pairs_ref, all_count_ref, low_ref)):
            copies.append(pltpu.make_async_remote_copy(
                src_ref=ref.at[rep], dst_ref=ref.at[rep],
                send_sem=rep_send.at[kind, step], recv_sem=rep_recv.at[kind, step],
                device_id={"rep": rep_peer(step, reps)},
            ))
        return copies

    @pl.loop(1, sites)
    def _(step):
        site_copy(step).start()

    base = half * far_cols
    for block in range(own):
        for part in range(BLOCK_LEN // LOW):
            low_ref[rep, block, :, part * LOW : (part + 1) * LOW] = pick(
                base + block * BLOCK_LEN + part * LOW
            )
    for step in range(1, reps):
        for copy in rep_copies(step):
            copy.start()
    base += own * BLOCK_LEN
    for block in range(own):
        for part in range(BLOCK_LEN // LOW):
            up_ref[block, :, part * LOW : (part + 1) * LOW] = pick(
                base + block * BLOCK_LEN + part * LOW
            )
    for step in range(1, reps):
        for copy in rep_copies(step):
            copy.wait()

    @pl.loop(1, sites)
    def _(step):
        site_copy(step).wait()


def three_pieces(value):
    first = value.astype(BF16).astype(F32)
    rest = value - first
    second = rest.astype(BF16).astype(F32)
    return first, second, rest - second


def norm_rows(norms, at, ones_at):
    row = lax.broadcasted_iota(jnp.int32, (16, norms.shape[1]), 0)
    rows = jnp.where((row >= ones_at) & (row < ones_at + 3), 1.0, 0.0)
    for place, piece in enumerate(three_pieces(norms)):
        rows = jnp.where(row == at + place, piece, rows)
    return rows


def right_form(points, scale_sq):
    pts = points.astype(F32)
    scaled = pts * scale_sq
    norms = jnp.sum(pts * scaled, axis=0, keepdims=True)
    rows = [*three_pieces(-2.0 * scaled), norm_rows(norms, 0, 3)]
    return jnp.concatenate(rows, axis=0).astype(BF16)


def left_form(points, scale_sq):
    pts = points.astype(F32)
    norms = jnp.sum(pts * (pts * scale_sq), axis=0, keepdims=True)
    rows = jnp.concatenate([pts, pts, pts, norm_rows(norms, 3, 0)], axis=0)
    return rows.T.astype(BF16)


def wendland(left, right):
    dist_sq = jnp.maximum(jnp.dot(left, right, preferred_element_type=F32), 1e-30)
    inside = jnp.maximum(1.0 - dist_sq * lax.rsqrt(dist_sq), 0.0)
    inside_sq = inside * inside
    return (inside_sq * inside_sq * (5.0 - 4.0 * inside)).astype(BF16)


def tile_kernel(
    pairs_ref, count_ref, scale_ref, low_ref, far_ref, up_ref,
    near_out, diag_out, far_out,
    rights, near_sum, far_sum, left, lists, fill,
):
    reps, _, slots = pairs_ref.shape
    near_total, width, _ = low_ref.shape
    far_total, _, cols = far_ref.shape
    own = up_ref.shape[0]
    feat_dim = scale_ref.shape[0]
    side_dim = width - feat_dim
    share = side_dim // reps
    half = near_total
    rep = lax.axis_index("rep")
    scale_sq = scale_ref[...] * scale_ref[...]

    for near in range(near_total):
        fill[near] = 0
    for owner in range(reps):
        @pl.loop(0, count_ref[owner, 0])
        def _(slot):
            near = lax.rem(pairs_ref[owner, 0, slot], 2 * half)
            far = pairs_ref[owner, 1, slot]
            seat = lax.div(far, 2 * half) * half + lax.rem(far, 2 * half) - half
            place = fill[near]
            lists[near, place] = seat
            fill[near] = place + 1
    for near in range(near_total):
        lists[near, fill[near]] = far_total

    @pl.loop(0, far_total)
    def _(far):
        rights[far] = right_form(far_ref[far, 0:feat_dim, :], scale_sq)
        far_sum[far] = jnp.zeros(far_sum.shape[1:], F32)

    rights[far_total] = jnp.zeros(rights.shape[1:], BF16)
    far_sum[far_total] = jnp.zeros(far_sum.shape[1:], F32)

    @pl.loop(0, near_total)
    def _(near):
        left[...] = left_form(low_ref[near, 0:feat_dim, :], scale_sq)
        near_sum[near] = jnp.zeros(near_sum.shape[1:], F32)
        near_vals = low_ref[near, feat_dim:width, :]

        @pl.loop(0, (fill[near] + 1) // 2)
        def _(step):
            one, two = lists[near, 2 * step], lists[near, 2 * step + 1]
            real_two = jnp.minimum(two, far_total - 1)
            keep = jnp.where(two < far_total, 1.0, 0.0).astype(BF16)
            right = jnp.concatenate([rights[one], rights[two]], axis=1)
            far_vals = jnp.concatenate(
                [far_ref[one, feat_dim:width, :], far_ref[real_two, feat_dim:width, :] * keep],
                axis=1,
            )
            toward_far = jnp.zeros((side_dim, 2 * cols), F32)
            for first in range(0, BLOCK_LEN, 256):
                rows = slice(first, first + 256)
                weights = wendland(left[rows, :], right)
                near_sum[near, :, rows] += lax.dot_general(
                    far_vals, weights, NT, preferred_element_type=F32
                )
                toward_far += jnp.dot(near_vals[:, rows], weights, preferred_element_type=F32)
            far_sum[one] += toward_far[:, :cols]
            far_sum[two] += toward_far[:, cols:]

    def diagonal(points, values):
        left[...] = left_form(points, scale_sq)
        right = right_form(points, scale_sq)
        parts = []
        for first in range(0, BLOCK_LEN, 256):
            part = jnp.zeros((side_dim, 256), F32)
            for top in range(0, BLOCK_LEN, 256):
                weights = wendland(left[top : top + 256, :], right[:, first : first + 256])
                part += jnp.dot(values[:, top : top + 256], weights, preferred_element_type=F32)
            parts.append(part)
        return jnp.concatenate(parts, axis=1)

    for block in range(own):
        near = rep * own + block
        near_sum[near] += diagonal(low_ref[near, 0:feat_dim, :], low_ref[near, feat_dim:width, :])
        total = diagonal(up_ref[block, 0:feat_dim, :], up_ref[block, feat_dim:width, :])
        for target in range(reps):
            diag_out[target, block * share : (block + 1) * share, :] = total[
                target * share : (target + 1) * share
            ]
    for near in range(near_total):
        total = near_sum[near]
        for target in range(reps):
            near_out[target, near * share : (near + 1) * share, :] = total[
                target * share : (target + 1) * share
            ].astype(LINK)

    @pl.loop(0, far_total // half)
    def _(home):
        totals = [far_sum[home * half + block] for block in range(half)]
        for target in range(reps):
            far_out[target, home] = jnp.concatenate(
                [total[target * share : (target + 1) * share] for total in totals], axis=0
            ).astype(LINK)


def place_kernel(
    sites, reps, near_ref, diag_ref, far_ref, order_ref, out_ref,
    near_got, diag_got, far_got, spots, near_send, near_recv, far_send, far_recv,
):
    site, rep = lax.axis_index("site"), lax.axis_index("rep")
    total_devices = sites * reps
    me = site * reps + rep
    site_len = order_ref.shape[1]
    high_total = site_len // LOW
    share = out_ref.shape[0] // high_total
    half = near_ref.shape[1] // share
    own = diag_ref.shape[1] // share
    cols = far_ref.shape[3]

    def peer(step):
        other = lax.rem(me + step, total_devices)
        return other // reps, lax.rem(other, reps)

    barrier = pltpu.get_barrier_semaphore()

    @pl.loop(1, total_devices)
    def _(step):
        to_site, to_rep = peer(step)
        pl.semaphore_signal(barrier, inc=1, device_id={"site": to_site, "rep": to_rep})

    near_got[rep] = near_ref[rep]
    diag_got[rep] = diag_ref[rep]
    far_got[site, rep] = far_ref[rep, site]
    pl.semaphore_wait(barrier, total_devices - 1)

    def far_copy(step):
        to_site, to_rep = peer(step)
        return pltpu.make_async_remote_copy(
            src_ref=far_ref.at[to_rep, to_site], dst_ref=far_got.at[site, rep],
            send_sem=far_send.at[step], recv_sem=far_recv.at[step],
            device_id={"site": to_site, "rep": to_rep},
        )

    def rep_copies(step):
        to_rep = rep_peer(step, reps)
        copies = []
        for kind, (src, dst) in enumerate(((near_ref, near_got), (diag_ref, diag_got))):
            copies.append(pltpu.make_async_remote_copy(
                src_ref=src.at[to_rep], dst_ref=dst.at[rep],
                send_sem=near_send.at[kind, step], recv_sem=near_recv.at[kind, step],
                device_id={"rep": to_rep},
            ))
        return copies

    @pl.loop(1, total_devices)
    def _(step):
        far_copy(step).start()

    for step in range(1, reps):
        for copy in rep_copies(step):
            copy.start()

    blocks = site_len // BLOCK_LEN
    for block in range(blocks):
        index = order_ref[:, block * BLOCK_LEN : (block + 1) * BLOCK_LEN]
        hit = lax.broadcasted_iota(jnp.int32, (LOW, BLOCK_LEN), 0) == index % LOW
        spots[block] = jnp.where(hit, 1.0, 0.0).astype(BF16)

    out_ref[...] = jnp.zeros(out_ref.shape, F32)

    def put(block, rows):
        index = order_ref[:, block * BLOCK_LEN : (block + 1) * BLOCK_LEN] // LOW
        hit = lax.broadcasted_iota(jnp.int32, (high_total, BLOCK_LEN), 0) == index
        spread = jnp.concatenate(
            [
                jnp.where(hit, jnp.broadcast_to(rows[k : k + 1], hit.shape), 0.0)
                for k in range(share)
            ],
            axis=0,
        )
        coarse = spread.astype(BF16)
        fine = (spread - coarse.astype(F32)).astype(BF16)
        out_ref[...] += lax.dot_general(
            coarse, spots[block], NT, preferred_element_type=F32
        ) + lax.dot_general(fine, spots[block], NT, preferred_element_type=F32)

    for step in range(1, reps):
        for copy in rep_copies(step):
            copy.wait()
    near_total = near_got[0].astype(F32)
    for source in range(1, reps):
        near_total += near_got[source].astype(F32)
    for block in range(half):
        put(block, near_total[block * share : (block + 1) * share])

    @pl.loop(1, total_devices)
    def _(step):
        far_copy(step).wait()

    parts = []
    for source in range(reps):
        def add(home, total, source=source):
            return total + far_got[home, source].astype(F32)
        parts.append(lax.fori_loop(0, sites, add, jnp.zeros((half * share, cols), F32)))
    far_total = jnp.concatenate(parts, axis=1)
    for block in range(half):
        inner = (block % own) * share
        put(
            half + block,
            far_total[block * share : (block + 1) * share]
            + diag_got[block // own, inner : inner + share, :],
        )


def shards(features, inverse_scale, right_sides, block_order, block_pairs, pair_count):
    sites, reps = lax.axis_size("site"), lax.axis_size("rep")
    rep = lax.axis_index("rep")
    feat_dim, site_len = features.shape
    side_dim = right_sides.shape[0]
    slots = block_pairs.shape[3]
    width = feat_dim + side_dim
    blocks = site_len // BLOCK_LEN
    half = blocks // 2
    own = half // reps
    cols = BLOCK_LEN // reps
    share = side_dim // reps
    far_total = sites * half
    limit = 48 * 2**20
    sem = pltpu.SemaphoreType.DMA

    order = block_order.reshape(blocks, BLOCK_LEN)
    mine = jnp.concatenate(
        [
            lax.dynamic_slice(order, (half, rep * cols), (half, cols)).reshape(1, -1),
            lax.dynamic_slice(block_order, (0, rep * own * BLOCK_LEN), (1, own * BLOCK_LEN)),
            lax.dynamic_slice(
                block_order, (0, (half + rep * own) * BLOCK_LEN), (1, own * BLOCK_LEN)
            ),
        ],
        axis=1,
    )
    low, far, up, pairs, counts = pl.pallas_call(
        functools.partial(collect_kernel, sites, reps),
        out_shape=(
            jax.ShapeDtypeStruct((reps, own, width, BLOCK_LEN), BF16),
            jax.ShapeDtypeStruct((sites, half, width, cols), BF16),
            jax.ShapeDtypeStruct((own, width, BLOCK_LEN), BF16),
            jax.ShapeDtypeStruct((reps, 2, slots), jnp.int32),
            jax.ShapeDtypeStruct((reps, 1, 1), jnp.int32),
        ),
        in_specs=[VMEM] * 5,
        out_specs=(VMEM,) * 5,
        scratch_shapes=[
            pltpu.VMEM((site_len // LOW * width, LOW), BF16),
            sem((3, reps)), sem((3, reps)), sem((sites,)), sem((sites,)),
        ],
        compiler_params=pltpu.CompilerParams(
            collective_id=0, has_side_effects=True, vmem_limit_bytes=limit
        ),
        name="collect",
    )(features, right_sides, mine, block_pairs.reshape(2, slots), pair_count)

    near_part, diag_part, far_part = pl.pallas_call(
        tile_kernel,
        out_shape=(
            jax.ShapeDtypeStruct((reps, half * share, BLOCK_LEN), LINK),
            jax.ShapeDtypeStruct((reps, own * share, BLOCK_LEN), F32),
            jax.ShapeDtypeStruct((reps, sites, half * share, cols), LINK),
        ),
        in_specs=[SMEM, SMEM] + [VMEM] * 4,
        out_specs=(VMEM,) * 3,
        scratch_shapes=[
            pltpu.VMEM((far_total + 1, DEPTH, cols), BF16),
            pltpu.VMEM((half, side_dim, BLOCK_LEN), F32),
            pltpu.VMEM((far_total + 1, side_dim, cols), F32),
            pltpu.VMEM((BLOCK_LEN, DEPTH), BF16),
            pltpu.SMEM((half, reps * slots + 2), jnp.int32),
            pltpu.SMEM((half,), jnp.int32),
        ],
        compiler_params=pltpu.CompilerParams(vmem_limit_bytes=limit),
        name="tiles",
    )(
        pairs,
        counts.reshape(reps, 1),
        inverse_scale.reshape(feat_dim, 1),
        low.reshape(half, width, BLOCK_LEN),
        far.reshape(far_total, width, cols),
        up,
    )

    placed = pl.pallas_call(
        functools.partial(place_kernel, sites, reps),
        out_shape=jax.ShapeDtypeStruct((share * (site_len // LOW), LOW), F32),
        in_specs=[VMEM] * 4,
        out_specs=VMEM,
        scratch_shapes=[
            pltpu.VMEM((reps, half * share, BLOCK_LEN), LINK),
            pltpu.VMEM((reps, own * share, BLOCK_LEN), F32),
            pltpu.VMEM((sites, reps, half * share, cols), LINK),
            pltpu.VMEM((blocks, LOW, BLOCK_LEN), BF16),
            sem((2, reps)), sem((2, reps)), sem((sites * reps,)), sem((sites * reps,)),
        ],
        compiler_params=pltpu.CompilerParams(
            collective_id=1, has_side_effects=True, vmem_limit_bytes=limit
        ),
        name="place",
    )(near_part, diag_part, far_part, block_order)
    return placed.reshape(share, site_len)


def solution(mesh):
    placed = (
        P(None, ("groups", "site")),
        P("groups"),
        P(None, ("groups", "site")),
        P(("groups", "site"), None),
        P(("groups", "site"), "rep", None, None),
        P(("groups", "site"), "rep"),
    )
    return jax.shard_map(
        shards, mesh=mesh, in_specs=placed, out_specs=P("rep", ("groups", "site")), check_vma=False
    )
```

```python
import functools

import jax
import jax.numpy as jnp
from jax import lax
from jax.experimental import pallas as pl
from jax.experimental.pallas import tpu as pltpu
from jax.sharding import PartitionSpec as P

BLOCK_LEN = 512
LOW = 256
DEPTH = 64
LINK = jnp.float32
UNROLL = 2
ROWS = 512
F32, BF16 = jnp.float32, jnp.bfloat16
VMEM = pl.BlockSpec(memory_space=pltpu.VMEM)
SMEM = pl.BlockSpec(memory_space=pltpu.SMEM)
HBM = pl.BlockSpec(memory_space=pltpu.HBM)
NT = (((1,), (1,)), ((), ()))


def rep_peer(step, reps):
    return lax.rem(lax.axis_index("rep") + step, reps)


def site_peer(step, sites):
    return lax.rem(lax.axis_index("site") + step, sites)


def collect_kernel(
    sites, reps, scale_ref, feat_hbm, side_hbm, order_hbm, pairs_hbm, count_hbm,
    low_ref, far_ref, all_pairs_ref, all_count_ref, low_diag_ref, up_diag_ref,
    feat_ref, side_ref, order_ref, stack, up_ref, load, rep_send, rep_recv, site_send, site_recv,
):
    site, rep = lax.axis_index("site"), lax.axis_index("rep")
    feat_dim, site_len = feat_ref.shape
    side_dim = side_ref.shape[0]
    width = feat_dim + side_dim
    share = side_dim // reps
    high_total = site_len // LOW
    cols = far_ref.shape[3]
    half = far_ref.shape[1]
    own = low_ref.shape[1]

    loads = [
        pltpu.make_async_copy(src, dst, load.at[place])
        for place, (src, dst) in enumerate((
            (order_hbm, order_ref), (feat_hbm, feat_ref), (side_hbm, side_ref),
            (pairs_hbm.at[0, 0], all_pairs_ref.at[rep]), (count_hbm, all_count_ref.at[rep]),
        ))
    ]
    for copy in loads:
        copy.start()

    barrier = pltpu.get_barrier_semaphore()
    for step in range(1, reps):
        pl.semaphore_signal(barrier, inc=1, device_id={"rep": rep_peer(step, reps)})

    @pl.loop(1, sites)
    def _(step):
        pl.semaphore_signal(barrier, inc=1, device_id={"site": site_peer(step, sites)})

    for copy in loads:
        copy.wait()

    for high in range(high_total):
        at = slice(high * LOW, (high + 1) * LOW)
        stack[high * width : high * width + feat_dim, :] = feat_ref[:, at]
        stack[high * width + feat_dim : (high + 1) * width, :] = side_ref[:, at]

    def pick(index):
        low = index % LOW
        high_part = index // LOW
        spot = lax.broadcasted_iota(jnp.int32, (LOW, LOW), 0) == low
        spot = jnp.where(spot, 1.0, 0.0).astype(BF16)
        picked = jnp.zeros((width, LOW), F32)
        group = 8
        for first in range(0, high_total, group):
            part = jnp.dot(
                stack[first * width : (first + group) * width, :], spot,
                preferred_element_type=F32,
            )
            for inner in range(group):
                hit = jnp.broadcast_to(high_part == first + inner, (width, LOW))
                picked = jnp.where(hit, part[inner * width : (inner + 1) * width], picked)
        return picked.astype(BF16)

    def own_part(block):
        start = block * BLOCK_LEN
        part = order_ref[:, start : start + cols]
        for other in range(1, reps):
            at = start + other * cols
            part = jnp.where(rep == other, order_ref[:, at : at + cols], part)
        return part

    def pick_block(block, put):
        for part in range(0, BLOCK_LEN, LOW):
            start = pl.multiple_of(block * BLOCK_LEN + part, LOW)
            put(slice(part, part + LOW), pick(order_ref[:, pl.ds(start, LOW)]))

    per_chunk = LOW // cols
    for first in range(0, half, per_chunk):
        blocks = range(first, first + per_chunk)
        picked = pick(jnp.concatenate([own_part(half + block) for block in blocks], axis=1))
        for inner, block in enumerate(blocks):
            far_ref[site, block] = picked[:, inner * cols : (inner + 1) * cols]

    pl.semaphore_wait(barrier, reps - 1 + sites - 1)

    def site_copy(step):
        return pltpu.make_async_remote_copy(
            src_ref=far_ref.at[site], dst_ref=far_ref.at[site],
            send_sem=site_send.at[step], recv_sem=site_recv.at[step],
            device_id={"site": site_peer(step, sites)},
        )

    def rep_copies(step):
        copies = []
        for kind, ref in enumerate((all_pairs_ref, all_count_ref, low_ref)):
            copies.append(pltpu.make_async_remote_copy(
                src_ref=ref.at[rep], dst_ref=ref.at[rep],
                send_sem=rep_send.at[kind, step], recv_sem=rep_recv.at[kind, step],
                device_id={"rep": rep_peer(step, reps)},
            ))
        return copies

    @pl.loop(1, sites)
    def _(step):
        site_copy(step).start()

    for block in range(own):
        def put_low(at, picked, block=block):
            low_ref[rep, block, :, at] = picked
        pick_block(rep * own + block, put_low)
    for step in range(1, reps):
        for copy in rep_copies(step):
            copy.start()
    for block in range(own):
        def put_up(at, picked, block=block):
            up_ref[block, :, at] = picked
        pick_block(half + rep * own + block, put_up)

    scale_sq = scale_column(scale_ref)

    def diagonal(points, values):
        left = left_form(points, scale_sq)
        right = right_form(points, scale_sq)
        parts = []
        for first in range(0, BLOCK_LEN, 256):
            weights = wendland(left, right[:, first : first + 256])
            parts.append(jnp.dot(values, weights, preferred_element_type=F32))
        return jnp.concatenate(parts, axis=1)

    for block in range(own):
        low_diag_ref[block] = diagonal(
            low_ref[rep, block, 0:feat_dim, :], low_ref[rep, block, feat_dim:width, :]
        )
        sums = diagonal(up_ref[block, 0:feat_dim, :], up_ref[block, feat_dim:width, :])
        for target in range(reps):
            up_diag_ref[target, block * share : (block + 1) * share, :] = sums[
                target * share : (target + 1) * share
            ]

    for step in range(1, reps):
        for copy in rep_copies(step):
            copy.wait()

    @pl.loop(1, sites)
    def _(step):
        site_copy(step).wait()


def scale_column(scale_ref):
    total = scale_ref.shape[1]
    row = lax.broadcasted_iota(jnp.int32, (total, total), 0)
    col = lax.broadcasted_iota(jnp.int32, (total, total), 1)
    spread = jnp.where(row == col, jnp.broadcast_to(scale_ref[...], (total, total)), 0.0)
    scale = jnp.sum(spread, axis=1, keepdims=True)
    return scale * scale


def three_pieces(value):
    first = value.astype(BF16).astype(F32)
    rest = value - first
    second = rest.astype(BF16).astype(F32)
    return first, second, rest - second


def norm_rows(norms, at, ones_at):
    row = lax.broadcasted_iota(jnp.int32, (16, norms.shape[1]), 0)
    rows = jnp.where((row >= ones_at) & (row < ones_at + 3), 1.0, 0.0)
    for place, piece in enumerate(three_pieces(norms)):
        rows = jnp.where(row == at + place, piece, rows)
    return rows


def right_form(points, scale_sq):
    pts = points.astype(F32)
    scaled = pts * scale_sq
    norms = jnp.sum(pts * scaled, axis=0, keepdims=True)
    rows = [*three_pieces(-2.0 * scaled), norm_rows(norms, 0, 3)]
    return jnp.concatenate(rows, axis=0).astype(BF16)


def left_form(points, scale_sq):
    pts = points.astype(F32)
    norms = jnp.sum(pts * (pts * scale_sq), axis=0, keepdims=True)
    rows = jnp.concatenate([pts, pts, pts, norm_rows(norms, 3, 0)], axis=0)
    return rows.T.astype(BF16)


def wendland(left, right):
    dist_sq = jnp.maximum(jnp.dot(left, right, preferred_element_type=F32), 1e-30)
    inside = jnp.maximum(1.0 - dist_sq * lax.rsqrt(dist_sq), 0.0)
    inside_sq = inside * inside
    return (inside_sq * inside_sq * (5.0 - 4.0 * inside)).astype(BF16)


def tile_kernel(
    pairs_ref, count_ref, scale_ref, low_ref, far_ref, diag_ref,
    near_out, far_out,
    rights, far_vals, lefts, near_sum, far_sum, chunk_near, seats, opened,
):
    reps, _, slots = pairs_ref.shape
    near_total, width, _ = low_ref.shape
    far_total, _, cols = far_ref.shape
    own = diag_ref.shape[0]
    feat_dim = scale_ref.shape[1]
    side_dim = width - feat_dim
    share = side_dim // reps
    half = near_total
    rep = lax.axis_index("rep")
    scale_sq = scale_column(scale_ref)

    for near in range(near_total):
        opened[near] = -1
    total = jnp.int32(0)
    for owner in range(reps):
        def enter(slot, total, owner=owner):
            near = lax.rem(pairs_ref[owner, 0, slot], 2 * half)
            far = pairs_ref[owner, 1, slot]
            seat = lax.div(far, 2 * half) * half + lax.rem(far, 2 * half) - half
            waiting = opened[near]
            fresh = waiting < 0
            chunk = jnp.where(fresh, total, waiting)
            chunk_near[chunk] = near
            seats[2 * chunk + 1] = jnp.where(fresh, far_total, seat)
            seats[2 * chunk] = jnp.where(fresh, seat, seats[2 * chunk])
            opened[near] = jnp.where(fresh, chunk, -1)
            return total + jnp.where(fresh, 1, 0)
        total = lax.fori_loop(0, count_ref[owner, 0, 0], enter, total)
    for extra in range(UNROLL - 1):
        chunk_near[total + extra] = 0
        seats[2 * (total + extra)] = far_total
        seats[2 * (total + extra) + 1] = far_total

    @pl.loop(0, far_total // half)
    def _(home):
        for block in range(half):
            far = home * half + block
            rights[far] = right_form(far_ref[far, 0:feat_dim, :], scale_sq)
            far_vals[far] = far_ref[far, feat_dim:width, :]
            far_sum[far] = jnp.zeros(far_sum.shape[1:], F32)

    rights[far_total] = jnp.zeros(rights.shape[1:], BF16)
    far_vals[far_total] = jnp.zeros(far_vals.shape[1:], BF16)
    far_sum[far_total] = jnp.zeros(far_sum.shape[1:], F32)

    near_sum[...] = jnp.zeros(near_sum.shape, F32)
    for block in range(own):
        near_sum[rep * own + block] = diag_ref[block]
    for near in range(near_total):
        lefts[near] = left_form(low_ref[near, 0:feat_dim, :], scale_sq)

    def run_chunks(chunks):
        pieces = []
        for chunk in chunks:
            near, one, two = chunk_near[chunk], seats[2 * chunk], seats[2 * chunk + 1]
            right = jnp.concatenate([rights[one], rights[two]], axis=1)
            vals = jnp.concatenate([far_vals[one], far_vals[two]], axis=1)
            near_vals = low_ref[near, feat_dim:width, :]
            toward_near, toward_far = [], jnp.zeros((side_dim, 2 * cols), F32)
            for first in range(0, BLOCK_LEN, ROWS):
                rows = slice(first, first + ROWS)
                weights = wendland(lefts[near, rows, :], right)
                toward_near.append(
                    lax.dot_general(vals, weights, NT, preferred_element_type=F32)
                )
                toward_far += jnp.dot(near_vals[:, rows], weights, preferred_element_type=F32)
            pieces.append((near, one, two, jnp.concatenate(toward_near, axis=1), toward_far))
        for near, one, two, toward_near, toward_far in pieces:
            near_sum[near] += toward_near
            far_sum[one] += toward_far[:, :cols]
            far_sum[two] += toward_far[:, cols:]

    @pl.loop(0, (total + UNROLL - 1) // UNROLL)
    def _(step):
        run_chunks([UNROLL * step + inner for inner in range(UNROLL)])

    for near in range(near_total):
        sums = near_sum[near]
        for target in range(reps):
            near_out[target, near * share : (near + 1) * share, :] = sums[
                target * share : (target + 1) * share
            ].astype(LINK)

    @pl.loop(0, far_total // half)
    def _(home):
        totals = [far_sum[home * half + block] for block in range(half)]
        for target in range(reps):
            far_out[target, home] = jnp.concatenate(
                [total[target * share : (target + 1) * share] for total in totals], axis=0
            ).astype(LINK)


def place_kernel(
    sites, reps, near_ref, diag_ref, far_ref, order_ref, out_ref,
    near_got, diag_got, far_got, spots, near_send, near_recv, far_send, far_recv,
):
    site, rep = lax.axis_index("site"), lax.axis_index("rep")
    total_devices = sites * reps
    me = site * reps + rep
    site_len = order_ref.shape[1]
    high_total = site_len // LOW
    share = out_ref.shape[0] // high_total
    half = near_ref.shape[1] // share
    own = diag_ref.shape[1] // share
    cols = far_ref.shape[3]

    def peer(step):
        other = lax.rem(me + step, total_devices)
        return other // reps, lax.rem(other, reps)

    barrier = pltpu.get_barrier_semaphore()

    @pl.loop(1, total_devices)
    def _(step):
        to_site, to_rep = peer(step)
        pl.semaphore_signal(barrier, inc=1, device_id={"site": to_site, "rep": to_rep})

    near_got[rep] = near_ref[rep]
    diag_got[rep] = diag_ref[rep]
    far_got[site, rep] = far_ref[rep, site]
    pl.semaphore_wait(barrier, total_devices - 1)

    def far_copy(step):
        to_site, to_rep = peer(step)
        return pltpu.make_async_remote_copy(
            src_ref=far_ref.at[to_rep, to_site], dst_ref=far_got.at[site, rep],
            send_sem=far_send.at[step], recv_sem=far_recv.at[step],
            device_id={"site": to_site, "rep": to_rep},
        )

    def rep_copies(step):
        to_rep = rep_peer(step, reps)
        copies = []
        for kind, (src, dst) in enumerate(((near_ref, near_got), (diag_ref, diag_got))):
            copies.append(pltpu.make_async_remote_copy(
                src_ref=src.at[to_rep], dst_ref=dst.at[rep],
                send_sem=near_send.at[kind, step], recv_sem=near_recv.at[kind, step],
                device_id={"rep": to_rep},
            ))
        return copies

    @pl.loop(1, total_devices)
    def _(step):
        far_copy(step).start()

    for step in range(1, reps):
        for copy in rep_copies(step):
            copy.start()

    blocks = site_len // BLOCK_LEN
    for block in range(blocks):
        index = order_ref[:, block * BLOCK_LEN : (block + 1) * BLOCK_LEN]
        hit = lax.broadcasted_iota(jnp.int32, (LOW, BLOCK_LEN), 0) == index % LOW
        spots[block] = jnp.where(hit, 1.0, 0.0).astype(BF16)

    out_ref[...] = jnp.zeros(out_ref.shape, F32)

    def put(block, rows):
        index = order_ref[:, block * BLOCK_LEN : (block + 1) * BLOCK_LEN] // LOW
        hit = lax.broadcasted_iota(jnp.int32, (high_total, BLOCK_LEN), 0) == index
        spread = jnp.concatenate(
            [
                jnp.where(hit, jnp.broadcast_to(rows[k : k + 1], hit.shape), 0.0)
                for k in range(share)
            ],
            axis=0,
        )
        coarse = spread.astype(BF16)
        fine = (spread - coarse.astype(F32)).astype(BF16)
        out_ref[...] += lax.dot_general(
            coarse, spots[block], NT, preferred_element_type=F32
        ) + lax.dot_general(fine, spots[block], NT, preferred_element_type=F32)

    for step in range(1, reps):
        for copy in rep_copies(step):
            copy.wait()
    near_total = near_got[0].astype(F32)
    for source in range(1, reps):
        near_total += near_got[source].astype(F32)
    for block in range(half):
        put(block, near_total[block * share : (block + 1) * share])

    @pl.loop(1, total_devices)
    def _(step):
        far_copy(step).wait()

    parts = []
    for source in range(reps):
        def add(home, total, source=source):
            return total + far_got[home, source].astype(F32)
        parts.append(lax.fori_loop(0, sites, add, jnp.zeros((half * share, cols), F32)))
    far_total = jnp.concatenate(parts, axis=1)
    for block in range(half):
        inner = (block % own) * share
        put(
            half + block,
            far_total[block * share : (block + 1) * share]
            + diag_got[block // own, inner : inner + share, :],
        )


def tiles_call(pairs, counts, scale, low, far, diag):
    reps, _, slots = pairs.shape
    half, width, _ = low.shape
    far_total, _, cols = far.shape
    side_dim = diag.shape[1]
    share = side_dim // reps
    return pl.pallas_call(
        tile_kernel,
        out_shape=(
            jax.ShapeDtypeStruct((reps, half * share, BLOCK_LEN), LINK),
            jax.ShapeDtypeStruct((reps, far_total // half, half * share, cols), LINK),
        ),
        in_specs=[SMEM, SMEM] + [VMEM] * 4,
        out_specs=(VMEM,) * 2,
        scratch_shapes=[
            pltpu.VMEM((far_total + 1, DEPTH, cols), BF16),
            pltpu.VMEM((far_total + 1, side_dim, cols), BF16),
            pltpu.VMEM((half, BLOCK_LEN, DEPTH), BF16),
            pltpu.VMEM((half, side_dim, BLOCK_LEN), F32),
            pltpu.VMEM((far_total + 1, side_dim, cols), F32),
            pltpu.SMEM((reps * slots + UNROLL,), jnp.int32),
            pltpu.SMEM((2 * (reps * slots + UNROLL),), jnp.int32),
            pltpu.SMEM((half,), jnp.int32),
        ],
        compiler_params=pltpu.CompilerParams(vmem_limit_bytes=48 * 2**20),
        name="tiles",
    )(pairs, counts, scale, low, far, diag)


def shards(features, inverse_scale, right_sides, block_order, block_pairs, pair_count):
    sites, reps = lax.axis_size("site"), lax.axis_size("rep")
    feat_dim, site_len = features.shape
    side_dim = right_sides.shape[0]
    slots = block_pairs.shape[3]
    width = feat_dim + side_dim
    blocks = site_len // BLOCK_LEN
    half = blocks // 2
    own = half // reps
    cols = BLOCK_LEN // reps
    share = side_dim // reps
    far_total = sites * half
    limit = 48 * 2**20
    sem = pltpu.SemaphoreType.DMA

    scale = inverse_scale.reshape(1, feat_dim)
    low, far, pairs, counts, low_diag, diag_part = pl.pallas_call(
        functools.partial(collect_kernel, sites, reps),
        out_shape=(
            jax.ShapeDtypeStruct((reps, own, width, BLOCK_LEN), BF16),
            jax.ShapeDtypeStruct((sites, half, width, cols), BF16),
            jax.ShapeDtypeStruct((reps, 2, slots), jnp.int32),
            jax.ShapeDtypeStruct((reps, 1, 1), jnp.int32),
            jax.ShapeDtypeStruct((own, side_dim, BLOCK_LEN), F32),
            jax.ShapeDtypeStruct((reps, own * share, BLOCK_LEN), F32),
        ),
        in_specs=[VMEM] + [HBM] * 5,
        out_specs=(VMEM,) * 6,
        scratch_shapes=[
            pltpu.VMEM(features.shape, BF16),
            pltpu.VMEM(right_sides.shape, BF16),
            pltpu.VMEM(block_order.shape, jnp.int32),
            pltpu.VMEM((site_len // LOW * width, LOW), BF16),
            pltpu.VMEM((own, width, BLOCK_LEN), BF16),
            sem((5,)), sem((3, reps)), sem((3, reps)), sem((sites,)), sem((sites,)),
        ],
        compiler_params=pltpu.CompilerParams(
            collective_id=0, has_side_effects=True, vmem_limit_bytes=limit
        ),
        name="collect",
    )(scale, features, right_sides, block_order, block_pairs, pair_count)

    near_part, far_part = tiles_call(
        pairs,
        counts,
        scale,
        low.reshape(half, width, BLOCK_LEN),
        far.reshape(far_total, width, cols),
        low_diag,
    )

    placed = pl.pallas_call(
        functools.partial(place_kernel, sites, reps),
        out_shape=jax.ShapeDtypeStruct((share * (site_len // LOW), LOW), F32),
        in_specs=[VMEM] * 4,
        out_specs=VMEM,
        scratch_shapes=[
            pltpu.VMEM((reps, half * share, BLOCK_LEN), LINK),
            pltpu.VMEM((reps, own * share, BLOCK_LEN), F32),
            pltpu.VMEM((sites, reps, half * share, cols), LINK),
            pltpu.VMEM((blocks, LOW, BLOCK_LEN), BF16),
            sem((2, reps)), sem((2, reps)), sem((sites * reps,)), sem((sites * reps,)),
        ],
        compiler_params=pltpu.CompilerParams(
            collective_id=1, has_side_effects=True, vmem_limit_bytes=limit
        ),
        name="place",
    )(near_part, diag_part, far_part, block_order)
    return placed.reshape(share, site_len)


def solution(mesh):
    placed = (
        P(None, ("groups", "site")),
        P("groups"),
        P(None, ("groups", "site")),
        P(("groups", "site"), None),
        P(("groups", "site"), "rep", None, None),
        P(("groups", "site"), "rep"),
    )
    return jax.shard_map(
        shards, mesh=mesh, in_specs=placed, out_specs=P("rep", ("groups", "site")), check_vma=False
    )
```

```python
import functools

import jax
import jax.numpy as jnp
from jax import lax
from jax.experimental import pallas as pl
from jax.experimental.pallas import tpu as pltpu
from jax.sharding import PartitionSpec as P

BLOCK_LEN = 512
LOW = 256
DEPTH = 64
LINK = jnp.bfloat16
UNROLL = 2
ROWS = 512
F32, BF16 = jnp.float32, jnp.bfloat16
VMEM = pl.BlockSpec(memory_space=pltpu.VMEM)
SMEM = pl.BlockSpec(memory_space=pltpu.SMEM)
HBM = pl.BlockSpec(memory_space=pltpu.HBM)
NT = (((1,), (1,)), ((), ()))


def rep_peer(step, reps):
    return lax.rem(lax.axis_index("rep") + step, reps)


def site_peer(step, sites):
    return lax.rem(lax.axis_index("site") + step, sites)


def collect_kernel(
    sites, reps, scale_ref, feat_hbm, side_hbm, order_hbm, pairs_hbm, count_hbm,
    low_ref, far_ref, all_pairs_ref, all_count_ref, low_diag_ref, up_diag_ref,
    feat_ref, side_ref, order_ref, stack, up_ref, load, rep_send, rep_recv, site_send, site_recv,
):
    site, rep = lax.axis_index("site"), lax.axis_index("rep")
    feat_dim, site_len = feat_ref.shape
    side_dim = side_ref.shape[0]
    width = feat_dim + side_dim
    share = side_dim // reps
    high_total = site_len // LOW
    cols = far_ref.shape[3]
    half = far_ref.shape[1]
    own = low_ref.shape[1]

    loads = [
        pltpu.make_async_copy(src, dst, load.at[place])
        for place, (src, dst) in enumerate((
            (order_hbm, order_ref), (feat_hbm, feat_ref), (side_hbm, side_ref),
            (pairs_hbm.at[0, 0], all_pairs_ref.at[rep]), (count_hbm, all_count_ref.at[rep]),
        ))
    ]
    for copy in loads:
        copy.start()

    barrier = pltpu.get_barrier_semaphore()
    for step in range(1, reps):
        pl.semaphore_signal(barrier, inc=1, device_id={"rep": rep_peer(step, reps)})

    @pl.loop(1, sites)
    def _(step):
        pl.semaphore_signal(barrier, inc=1, device_id={"site": site_peer(step, sites)})

    for copy in loads:
        copy.wait()

    for high in range(high_total):
        at = slice(high * LOW, (high + 1) * LOW)
        stack[high * width : high * width + feat_dim, :] = feat_ref[:, at]
        stack[high * width + feat_dim : (high + 1) * width, :] = side_ref[:, at]

    def pick(index):
        low = index % LOW
        high_part = index // LOW
        spot = lax.broadcasted_iota(jnp.int32, (LOW, LOW), 0) == low
        spot = jnp.where(spot, 1.0, 0.0).astype(BF16)
        picked = jnp.zeros((width, LOW), F32)
        group = 8
        for first in range(0, high_total, group):
            part = jnp.dot(
                stack[first * width : (first + group) * width, :], spot,
                preferred_element_type=F32,
            )
            for inner in range(group):
                hit = jnp.broadcast_to(high_part == first + inner, (width, LOW))
                picked = jnp.where(hit, part[inner * width : (inner + 1) * width], picked)
        return picked.astype(BF16)

    def own_part(block):
        start = block * BLOCK_LEN
        part = order_ref[:, start : start + cols]
        for other in range(1, reps):
            at = start + other * cols
            part = jnp.where(rep == other, order_ref[:, at : at + cols], part)
        return part

    def pick_block(block, put):
        for part in range(0, BLOCK_LEN, LOW):
            start = pl.multiple_of(block * BLOCK_LEN + part, LOW)
            put(slice(part, part + LOW), pick(order_ref[:, pl.ds(start, LOW)]))

    per_chunk = LOW // cols
    for first in range(0, half, per_chunk):
        blocks = range(first, first + per_chunk)
        picked = pick(jnp.concatenate([own_part(half + block) for block in blocks], axis=1))
        for inner, block in enumerate(blocks):
            far_ref[site, block] = picked[:, inner * cols : (inner + 1) * cols]

    pl.semaphore_wait(barrier, reps - 1 + sites - 1)

    def site_copy(step):
        return pltpu.make_async_remote_copy(
            src_ref=far_ref.at[site], dst_ref=far_ref.at[site],
            send_sem=site_send.at[step], recv_sem=site_recv.at[step],
            device_id={"site": site_peer(step, sites)},
        )

    def rep_copies(step):
        copies = []
        for kind, ref in enumerate((all_pairs_ref, all_count_ref, low_ref)):
            copies.append(pltpu.make_async_remote_copy(
                src_ref=ref.at[rep], dst_ref=ref.at[rep],
                send_sem=rep_send.at[kind, step], recv_sem=rep_recv.at[kind, step],
                device_id={"rep": rep_peer(step, reps)},
            ))
        return copies

    @pl.loop(1, sites)
    def _(step):
        site_copy(step).start()

    for block in range(own):
        def put_low(at, picked, block=block):
            low_ref[rep, block, :, at] = picked
        pick_block(rep * own + block, put_low)
    for step in range(1, reps):
        for copy in rep_copies(step):
            copy.start()
    for block in range(own):
        def put_up(at, picked, block=block):
            up_ref[block, :, at] = picked
        pick_block(half + rep * own + block, put_up)

    scale_sq = scale_column(scale_ref)

    def diagonal(points, values):
        left = left_form(points, scale_sq)
        right = right_form(points, scale_sq)
        parts = []
        for first in range(0, BLOCK_LEN, 256):
            weights = wendland(left, right[:, first : first + 256])
            parts.append(jnp.dot(values, weights, preferred_element_type=F32))
        return jnp.concatenate(parts, axis=1)

    for block in range(own):
        low_diag_ref[block] = diagonal(
            low_ref[rep, block, 0:feat_dim, :], low_ref[rep, block, feat_dim:width, :]
        )
        sums = diagonal(up_ref[block, 0:feat_dim, :], up_ref[block, feat_dim:width, :])
        for target in range(reps):
            up_diag_ref[target, block * share : (block + 1) * share, :] = sums[
                target * share : (target + 1) * share
            ]

    for step in range(1, reps):
        for copy in rep_copies(step):
            copy.wait()

    @pl.loop(1, sites)
    def _(step):
        site_copy(step).wait()


def scale_column(scale_ref):
    total = scale_ref.shape[1]
    row = lax.broadcasted_iota(jnp.int32, (total, total), 0)
    col = lax.broadcasted_iota(jnp.int32, (total, total), 1)
    spread = jnp.where(row == col, jnp.broadcast_to(scale_ref[...], (total, total)), 0.0)
    scale = jnp.sum(spread, axis=1, keepdims=True)
    return scale * scale


def three_pieces(value):
    first = value.astype(BF16).astype(F32)
    rest = value - first
    second = rest.astype(BF16).astype(F32)
    return first, second, rest - second


def norm_rows(norms, at, ones_at):
    row = lax.broadcasted_iota(jnp.int32, (16, norms.shape[1]), 0)
    rows = jnp.where((row >= ones_at) & (row < ones_at + 3), 1.0, 0.0)
    for place, piece in enumerate(three_pieces(norms)):
        rows = jnp.where(row == at + place, piece, rows)
    return rows


def right_form(points, scale_sq):
    pts = points.astype(F32)
    scaled = pts * scale_sq
    norms = jnp.sum(pts * scaled, axis=0, keepdims=True)
    rows = [*three_pieces(-2.0 * scaled), norm_rows(norms, 0, 3)]
    return jnp.concatenate(rows, axis=0).astype(BF16)


def left_form(points, scale_sq):
    pts = points.astype(F32)
    norms = jnp.sum(pts * (pts * scale_sq), axis=0, keepdims=True)
    rows = jnp.concatenate([pts, pts, pts, norm_rows(norms, 3, 0)], axis=0)
    return rows.T.astype(BF16)


def wendland(left, right):
    dist_sq = jnp.maximum(jnp.dot(left, right, preferred_element_type=F32), 1e-30)
    inside = jnp.maximum(1.0 - dist_sq * lax.rsqrt(dist_sq), 0.0)
    inside_sq = inside * inside
    return (inside_sq * inside_sq * (5.0 - 4.0 * inside)).astype(BF16)


def tile_kernel(
    pairs_ref, count_ref, scale_ref, low_ref, far_ref, diag_ref,
    near_out, far_out,
    rights, far_vals, lefts, near_sum, far_sum, chunk_near, seats, opened,
):
    reps, _, slots = pairs_ref.shape
    near_total, width, _ = low_ref.shape
    far_total, _, cols = far_ref.shape
    own = diag_ref.shape[0]
    feat_dim = scale_ref.shape[1]
    side_dim = width - feat_dim
    share = side_dim // reps
    half = near_total
    rep = lax.axis_index("rep")
    scale_sq = scale_column(scale_ref)

    for near in range(near_total):
        opened[near] = -1
    total = jnp.int32(0)
    for owner in range(reps):
        def enter(slot, total, owner=owner):
            near = lax.rem(pairs_ref[owner, 0, slot], 2 * half)
            far = pairs_ref[owner, 1, slot]
            seat = lax.div(far, 2 * half) * half + lax.rem(far, 2 * half) - half
            waiting = opened[near]
            fresh = waiting < 0
            chunk = jnp.where(fresh, total, waiting)
            chunk_near[chunk] = near
            seats[2 * chunk + 1] = jnp.where(fresh, far_total, seat)
            seats[2 * chunk] = jnp.where(fresh, seat, seats[2 * chunk])
            opened[near] = jnp.where(fresh, chunk, -1)
            return total + jnp.where(fresh, 1, 0)
        total = lax.fori_loop(0, count_ref[owner, 0, 0], enter, total)
    for extra in range(UNROLL - 1):
        chunk_near[total + extra] = 0
        seats[2 * (total + extra)] = far_total
        seats[2 * (total + extra) + 1] = far_total

    @pl.loop(0, far_total // half)
    def _(home):
        for block in range(half):
            far = home * half + block
            rights[far] = right_form(far_ref[far, 0:feat_dim, :], scale_sq)
            far_vals[far] = far_ref[far, feat_dim:width, :]
            far_sum[far] = jnp.zeros(far_sum.shape[1:], F32)

    rights[far_total] = jnp.zeros(rights.shape[1:], BF16)
    far_vals[far_total] = jnp.zeros(far_vals.shape[1:], BF16)
    far_sum[far_total] = jnp.zeros(far_sum.shape[1:], F32)

    near_sum[...] = jnp.zeros(near_sum.shape, F32)
    for block in range(own):
        near_sum[rep * own + block] = diag_ref[block]
    for near in range(near_total):
        lefts[near] = left_form(low_ref[near, 0:feat_dim, :], scale_sq)

    def run_chunks(chunks):
        pieces = []
        for chunk in chunks:
            near, one, two = chunk_near[chunk], seats[2 * chunk], seats[2 * chunk + 1]
            right = jnp.concatenate([rights[one], rights[two]], axis=1)
            vals = jnp.concatenate([far_vals[one], far_vals[two]], axis=1)
            near_vals = low_ref[near, feat_dim:width, :]
            toward_near, toward_far = [], jnp.zeros((side_dim, 2 * cols), F32)
            for first in range(0, BLOCK_LEN, ROWS):
                rows = slice(first, first + ROWS)
                weights = wendland(lefts[near, rows, :], right)
                toward_near.append(
                    lax.dot_general(vals, weights, NT, preferred_element_type=F32)
                )
                toward_far += jnp.dot(near_vals[:, rows], weights, preferred_element_type=F32)
            pieces.append((near, one, two, jnp.concatenate(toward_near, axis=1), toward_far))
        for near, one, two, toward_near, toward_far in pieces:
            near_sum[near] += toward_near
            far_sum[one] += toward_far[:, :cols]
            far_sum[two] += toward_far[:, cols:]

    @pl.loop(0, (total + UNROLL - 1) // UNROLL)
    def _(step):
        run_chunks([UNROLL * step + inner for inner in range(UNROLL)])

    for near in range(near_total):
        sums = near_sum[near]
        for target in range(reps):
            near_out[target, near * share : (near + 1) * share, :] = sums[
                target * share : (target + 1) * share
            ].astype(LINK)

    @pl.loop(0, far_total // half)
    def _(home):
        totals = [far_sum[home * half + block] for block in range(half)]
        for target in range(reps):
            far_out[target, home] = jnp.concatenate(
                [total[target * share : (target + 1) * share] for total in totals], axis=0
            ).astype(LINK)


def place_kernel(
    sites, reps, near_ref, diag_ref, far_ref, order_ref, out_ref,
    near_got, diag_got, far_got, spots, near_send, near_recv, far_send, far_recv,
):
    site, rep = lax.axis_index("site"), lax.axis_index("rep")
    total_devices = sites * reps
    me = site * reps + rep
    site_len = order_ref.shape[1]
    high_total = site_len // LOW
    share = out_ref.shape[0] // high_total
    half = near_ref.shape[1] // share
    own = diag_ref.shape[1] // share
    cols = far_ref.shape[3]

    def peer(step):
        other = lax.rem(me + step, total_devices)
        return other // reps, lax.rem(other, reps)

    barrier = pltpu.get_barrier_semaphore()

    @pl.loop(1, total_devices)
    def _(step):
        to_site, to_rep = peer(step)
        pl.semaphore_signal(barrier, inc=1, device_id={"site": to_site, "rep": to_rep})

    near_got[rep] = near_ref[rep]
    diag_got[rep] = diag_ref[rep]
    far_got[site, rep] = far_ref[rep, site]
    pl.semaphore_wait(barrier, total_devices - 1)

    def far_copy(step):
        to_site, to_rep = peer(step)
        return pltpu.make_async_remote_copy(
            src_ref=far_ref.at[to_rep, to_site], dst_ref=far_got.at[site, rep],
            send_sem=far_send.at[step], recv_sem=far_recv.at[step],
            device_id={"site": to_site, "rep": to_rep},
        )

    def rep_copies(step):
        to_rep = rep_peer(step, reps)
        copies = []
        for kind, (src, dst) in enumerate(((near_ref, near_got), (diag_ref, diag_got))):
            copies.append(pltpu.make_async_remote_copy(
                src_ref=src.at[to_rep], dst_ref=dst.at[rep],
                send_sem=near_send.at[kind, step], recv_sem=near_recv.at[kind, step],
                device_id={"rep": to_rep},
            ))
        return copies

    @pl.loop(1, total_devices)
    def _(step):
        far_copy(step).start()

    for step in range(1, reps):
        for copy in rep_copies(step):
            copy.start()

    blocks = site_len // BLOCK_LEN
    for block in range(blocks):
        index = order_ref[:, block * BLOCK_LEN : (block + 1) * BLOCK_LEN]
        hit = lax.broadcasted_iota(jnp.int32, (LOW, BLOCK_LEN), 0) == index % LOW
        spots[block] = jnp.where(hit, 1.0, 0.0).astype(BF16)

    out_ref[...] = jnp.zeros(out_ref.shape, F32)

    def put(block, rows):
        index = order_ref[:, block * BLOCK_LEN : (block + 1) * BLOCK_LEN] // LOW
        hit = lax.broadcasted_iota(jnp.int32, (high_total, BLOCK_LEN), 0) == index
        spread = jnp.concatenate(
            [
                jnp.where(hit, jnp.broadcast_to(rows[k : k + 1], hit.shape), 0.0)
                for k in range(share)
            ],
            axis=0,
        )
        coarse = spread.astype(BF16)
        fine = (spread - coarse.astype(F32)).astype(BF16)
        both = lax.dot_general(
            jnp.concatenate([coarse, fine], axis=0), spots[block], NT, preferred_element_type=F32
        )
        out_ref[...] += both[: spread.shape[0]] + both[spread.shape[0] :]

    for step in range(1, reps):
        for copy in rep_copies(step):
            copy.wait()
    near_total = near_got[0].astype(F32)
    for source in range(1, reps):
        near_total += near_got[source].astype(F32)
    for block in range(half):
        put(block, near_total[block * share : (block + 1) * share])

    @pl.loop(1, total_devices)
    def _(step):
        far_copy(step).wait()

    parts = []
    for source in range(reps):
        def add(home, total, source=source):
            return total + far_got[home, source].astype(F32)
        parts.append(lax.fori_loop(0, sites, add, jnp.zeros((half * share, cols), F32)))
    far_total = jnp.concatenate(parts, axis=1)
    for block in range(half):
        inner = (block % own) * share
        put(
            half + block,
            far_total[block * share : (block + 1) * share]
            + diag_got[block // own, inner : inner + share, :],
        )


def tiles_call(pairs, counts, scale, low, far, diag):
    reps, _, slots = pairs.shape
    half, width, _ = low.shape
    far_total, _, cols = far.shape
    side_dim = diag.shape[1]
    share = side_dim // reps
    return pl.pallas_call(
        tile_kernel,
        out_shape=(
            jax.ShapeDtypeStruct((reps, half * share, BLOCK_LEN), LINK),
            jax.ShapeDtypeStruct((reps, far_total // half, half * share, cols), LINK),
        ),
        in_specs=[SMEM, SMEM] + [VMEM] * 4,
        out_specs=(VMEM,) * 2,
        scratch_shapes=[
            pltpu.VMEM((far_total + 1, DEPTH, cols), BF16),
            pltpu.VMEM((far_total + 1, side_dim, cols), BF16),
            pltpu.VMEM((half, BLOCK_LEN, DEPTH), BF16),
            pltpu.VMEM((half, side_dim, BLOCK_LEN), F32),
            pltpu.VMEM((far_total + 1, side_dim, cols), F32),
            pltpu.SMEM((reps * slots + UNROLL,), jnp.int32),
            pltpu.SMEM((2 * (reps * slots + UNROLL),), jnp.int32),
            pltpu.SMEM((half,), jnp.int32),
        ],
        compiler_params=pltpu.CompilerParams(vmem_limit_bytes=48 * 2**20),
        name="tiles",
    )(pairs, counts, scale, low, far, diag)


def shards(features, inverse_scale, right_sides, block_order, block_pairs, pair_count):
    sites, reps = lax.axis_size("site"), lax.axis_size("rep")
    feat_dim, site_len = features.shape
    side_dim = right_sides.shape[0]
    slots = block_pairs.shape[3]
    width = feat_dim + side_dim
    blocks = site_len // BLOCK_LEN
    half = blocks // 2
    own = half // reps
    cols = BLOCK_LEN // reps
    share = side_dim // reps
    far_total = sites * half
    limit = 48 * 2**20
    sem = pltpu.SemaphoreType.DMA

    scale = inverse_scale.reshape(1, feat_dim)
    low, far, pairs, counts, low_diag, diag_part = pl.pallas_call(
        functools.partial(collect_kernel, sites, reps),
        out_shape=(
            jax.ShapeDtypeStruct((reps, own, width, BLOCK_LEN), BF16),
            jax.ShapeDtypeStruct((sites, half, width, cols), BF16),
            jax.ShapeDtypeStruct((reps, 2, slots), jnp.int32),
            jax.ShapeDtypeStruct((reps, 1, 1), jnp.int32),
            jax.ShapeDtypeStruct((own, side_dim, BLOCK_LEN), F32),
            jax.ShapeDtypeStruct((reps, own * share, BLOCK_LEN), F32),
        ),
        in_specs=[VMEM] + [HBM] * 5,
        out_specs=(VMEM,) * 6,
        scratch_shapes=[
            pltpu.VMEM(features.shape, BF16),
            pltpu.VMEM(right_sides.shape, BF16),
            pltpu.VMEM(block_order.shape, jnp.int32),
            pltpu.VMEM((site_len // LOW * width, LOW), BF16),
            pltpu.VMEM((own, width, BLOCK_LEN), BF16),
            sem((5,)), sem((3, reps)), sem((3, reps)), sem((sites,)), sem((sites,)),
        ],
        compiler_params=pltpu.CompilerParams(
            collective_id=0, has_side_effects=True, vmem_limit_bytes=limit
        ),
        name="collect",
    )(scale, features, right_sides, block_order, block_pairs, pair_count)

    near_part, far_part = tiles_call(
        pairs,
        counts,
        scale,
        low.reshape(half, width, BLOCK_LEN),
        far.reshape(far_total, width, cols),
        low_diag,
    )

    placed = pl.pallas_call(
        functools.partial(place_kernel, sites, reps),
        out_shape=jax.ShapeDtypeStruct((share * (site_len // LOW), LOW), F32),
        in_specs=[VMEM] * 4,
        out_specs=VMEM,
        scratch_shapes=[
            pltpu.VMEM((reps, half * share, BLOCK_LEN), LINK),
            pltpu.VMEM((reps, own * share, BLOCK_LEN), F32),
            pltpu.VMEM((sites, reps, half * share, cols), LINK),
            pltpu.VMEM((blocks, LOW, BLOCK_LEN), BF16),
            sem((2, reps)), sem((2, reps)), sem((sites * reps,)), sem((sites * reps,)),
        ],
        compiler_params=pltpu.CompilerParams(
            collective_id=1, has_side_effects=True, vmem_limit_bytes=limit
        ),
        name="place",
    )(near_part, diag_part, far_part, block_order)
    return placed.reshape(share, site_len)


def solution(mesh):
    placed = (
        P(None, ("groups", "site")),
        P("groups"),
        P(None, ("groups", "site")),
        P(("groups", "site"), None),
        P(("groups", "site"), "rep", None, None),
        P(("groups", "site"), "rep"),
    )
    return jax.shard_map(
        shards, mesh=mesh, in_specs=placed, out_specs=P("rep", ("groups", "site")), check_vma=False
    )
```

```python
import functools

import jax
import jax.numpy as jnp
from jax import lax
from jax.experimental import pallas as pl
from jax.experimental.pallas import tpu as pltpu
from jax.sharding import PartitionSpec as P

BLOCK_LEN = 512
LOW = 256
DEPTH = 64
LINK = jnp.bfloat16
UNROLL = 4
ROWS = 512
F32, BF16 = jnp.float32, jnp.bfloat16
VMEM = pl.BlockSpec(memory_space=pltpu.VMEM)
SMEM = pl.BlockSpec(memory_space=pltpu.SMEM)
HBM = pl.BlockSpec(memory_space=pltpu.HBM)
NT = (((1,), (1,)), ((), ()))


def rep_peer(step, reps):
    return lax.rem(lax.axis_index("rep") + step, reps)


def site_peer(step, sites):
    return lax.rem(lax.axis_index("site") + step, sites)


def collect_kernel(
    sites, reps, scale_ref, feat_hbm, side_hbm, order_hbm, pairs_hbm, count_hbm,
    low_ref, far_ref, all_pairs_ref, all_count_ref, low_diag_ref, up_diag_ref,
    feat_ref, side_ref, order_ref, stack, up_ref, load, rep_send, rep_recv, site_send, site_recv,
):
    site, rep = lax.axis_index("site"), lax.axis_index("rep")
    feat_dim, site_len = feat_ref.shape
    side_dim = side_ref.shape[0]
    width = feat_dim + side_dim
    share = side_dim // reps
    high_total = site_len // LOW
    cols = far_ref.shape[3]
    half = far_ref.shape[1]
    own = low_ref.shape[1]

    loads = [
        pltpu.make_async_copy(src, dst, load.at[place])
        for place, (src, dst) in enumerate((
            (order_hbm, order_ref), (feat_hbm, feat_ref), (side_hbm, side_ref),
            (pairs_hbm.at[0, 0], all_pairs_ref.at[rep]), (count_hbm, all_count_ref.at[rep]),
        ))
    ]
    for copy in loads:
        copy.start()

    barrier = pltpu.get_barrier_semaphore()
    for step in range(1, reps):
        pl.semaphore_signal(barrier, inc=1, device_id={"rep": rep_peer(step, reps)})

    @pl.loop(1, sites)
    def _(step):
        pl.semaphore_signal(barrier, inc=1, device_id={"site": site_peer(step, sites)})

    for copy in loads:
        copy.wait()

    for high in range(high_total):
        at = slice(high * LOW, (high + 1) * LOW)
        stack[high * width : high * width + feat_dim, :] = feat_ref[:, at]
        stack[high * width + feat_dim : (high + 1) * width, :] = side_ref[:, at]

    def pick(index):
        low = index % LOW
        high_part = index // LOW
        spot = lax.broadcasted_iota(jnp.int32, (LOW, LOW), 0) == low
        spot = jnp.where(spot, 1.0, 0.0).astype(BF16)
        picked = jnp.zeros((width, LOW), F32)
        group = 8
        for first in range(0, high_total, group):
            part = jnp.dot(
                stack[first * width : (first + group) * width, :], spot,
                preferred_element_type=F32,
            )
            for inner in range(group):
                hit = jnp.broadcast_to(high_part == first + inner, (width, LOW))
                picked = jnp.where(hit, part[inner * width : (inner + 1) * width], picked)
        return picked.astype(BF16)

    def own_part(block):
        start = block * BLOCK_LEN
        part = order_ref[:, start : start + cols]
        for other in range(1, reps):
            at = start + other * cols
            part = jnp.where(rep == other, order_ref[:, at : at + cols], part)
        return part

    def pick_block(block, put):
        for part in range(0, BLOCK_LEN, LOW):
            start = pl.multiple_of(block * BLOCK_LEN + part, LOW)
            put(slice(part, part + LOW), pick(order_ref[:, pl.ds(start, LOW)]))

    per_chunk = LOW // cols
    for first in range(0, half, per_chunk):
        blocks = range(first, first + per_chunk)
        picked = pick(jnp.concatenate([own_part(half + block) for block in blocks], axis=1))
        for inner, block in enumerate(blocks):
            far_ref[site, block] = picked[:, inner * cols : (inner + 1) * cols]

    pl.semaphore_wait(barrier, reps - 1 + sites - 1)

    def site_copy(step):
        return pltpu.make_async_remote_copy(
            src_ref=far_ref.at[site], dst_ref=far_ref.at[site],
            send_sem=site_send.at[step], recv_sem=site_recv.at[step],
            device_id={"site": site_peer(step, sites)},
        )

    def rep_copies(step):
        copies = []
        for kind, ref in enumerate((all_pairs_ref, all_count_ref, low_ref)):
            copies.append(pltpu.make_async_remote_copy(
                src_ref=ref.at[rep], dst_ref=ref.at[rep],
                send_sem=rep_send.at[kind, step], recv_sem=rep_recv.at[kind, step],
                device_id={"rep": rep_peer(step, reps)},
            ))
        return copies

    @pl.loop(1, sites)
    def _(step):
        site_copy(step).start()

    for block in range(own):
        def put_low(at, picked, block=block):
            low_ref[rep, block, :, at] = picked
        pick_block(rep * own + block, put_low)
    for step in range(1, reps):
        for copy in rep_copies(step):
            copy.start()
    for block in range(own):
        def put_up(at, picked, block=block):
            up_ref[block, :, at] = picked
        pick_block(half + rep * own + block, put_up)

    scale_sq = scale_column(scale_ref)

    def diagonal(points, values):
        left = left_form(points, scale_sq)
        right = right_form(points, scale_sq)
        parts = []
        for first in range(0, BLOCK_LEN, 256):
            weights = wendland(left, right[:, first : first + 256])
            parts.append(jnp.dot(values, weights, preferred_element_type=F32))
        return jnp.concatenate(parts, axis=1)

    for block in range(own):
        low_diag_ref[block] = diagonal(
            low_ref[rep, block, 0:feat_dim, :], low_ref[rep, block, feat_dim:width, :]
        )
        sums = diagonal(up_ref[block, 0:feat_dim, :], up_ref[block, feat_dim:width, :])
        for target in range(reps):
            up_diag_ref[target, block * share : (block + 1) * share, :] = sums[
                target * share : (target + 1) * share
            ]

    for step in range(1, reps):
        for copy in rep_copies(step):
            copy.wait()

    @pl.loop(1, sites)
    def _(step):
        site_copy(step).wait()


def scale_column(scale_ref):
    total = scale_ref.shape[1]
    row = lax.broadcasted_iota(jnp.int32, (total, total), 0)
    col = lax.broadcasted_iota(jnp.int32, (total, total), 1)
    spread = jnp.where(row == col, jnp.broadcast_to(scale_ref[...], (total, total)), 0.0)
    scale = jnp.sum(spread, axis=1, keepdims=True)
    return scale * scale


def three_pieces(value):
    first = value.astype(BF16).astype(F32)
    rest = value - first
    second = rest.astype(BF16).astype(F32)
    return first, second, rest - second


def norm_rows(norms, at, ones_at):
    row = lax.broadcasted_iota(jnp.int32, (16, norms.shape[1]), 0)
    rows = jnp.where((row >= ones_at) & (row < ones_at + 3), 1.0, 0.0)
    for place, piece in enumerate(three_pieces(norms)):
        rows = jnp.where(row == at + place, piece, rows)
    return rows


def right_form(points, scale_sq):
    pts = points.astype(F32)
    scaled = pts * scale_sq
    norms = jnp.sum(pts * scaled, axis=0, keepdims=True)
    rows = [*three_pieces(-2.0 * scaled), norm_rows(norms, 0, 3)]
    return jnp.concatenate(rows, axis=0).astype(BF16)


def left_form(points, scale_sq):
    pts = points.astype(F32)
    norms = jnp.sum(pts * (pts * scale_sq), axis=0, keepdims=True)
    rows = jnp.concatenate([pts, pts, pts, norm_rows(norms, 3, 0)], axis=0)
    return rows.T.astype(BF16)


def wendland(left, right):
    dist_sq = jnp.maximum(jnp.dot(left, right, preferred_element_type=F32), 1e-30)
    inside = jnp.maximum(1.0 - dist_sq * lax.rsqrt(dist_sq), 0.0)
    inside_sq = inside * inside
    return (inside_sq * inside_sq * (5.0 - 4.0 * inside)).astype(BF16)


def tile_kernel(
    pairs_ref, count_ref, scale_ref, low_ref, far_ref, diag_ref,
    near_out, far_out,
    rights, far_vals, lefts, near_sum, far_sum, chunk_near, seats, opened,
):
    reps, _, slots = pairs_ref.shape
    near_total, width, _ = low_ref.shape
    far_total, _, cols = far_ref.shape
    own = diag_ref.shape[0]
    feat_dim = scale_ref.shape[1]
    side_dim = width - feat_dim
    share = side_dim // reps
    half = near_total
    rep = lax.axis_index("rep")
    scale_sq = scale_column(scale_ref)

    for near in range(near_total):
        opened[near] = -1
    total = jnp.int32(0)
    for owner in range(reps):
        def enter(slot, total, owner=owner):
            near = lax.rem(pairs_ref[owner, 0, slot], 2 * half)
            far = pairs_ref[owner, 1, slot]
            seat = lax.div(far, 2 * half) * half + lax.rem(far, 2 * half) - half
            waiting = opened[near]
            fresh = waiting < 0
            chunk = jnp.where(fresh, total, waiting)
            chunk_near[chunk] = near
            seats[2 * chunk + 1] = jnp.where(fresh, far_total, seat)
            seats[2 * chunk] = jnp.where(fresh, seat, seats[2 * chunk])
            opened[near] = jnp.where(fresh, chunk, -1)
            return total + jnp.where(fresh, 1, 0)
        total = lax.fori_loop(0, count_ref[owner, 0, 0], enter, total)
    for extra in range(UNROLL - 1):
        chunk_near[total + extra] = 0
        seats[2 * (total + extra)] = far_total
        seats[2 * (total + extra) + 1] = far_total

    @pl.loop(0, far_total // half)
    def _(home):
        for block in range(half):
            far = home * half + block
            rights[far] = right_form(far_ref[far, 0:feat_dim, :], scale_sq)
            far_vals[far] = far_ref[far, feat_dim:width, :]
            far_sum[far] = jnp.zeros(far_sum.shape[1:], F32)

    rights[far_total] = jnp.zeros(rights.shape[1:], BF16)
    far_vals[far_total] = jnp.zeros(far_vals.shape[1:], BF16)
    far_sum[far_total] = jnp.zeros(far_sum.shape[1:], F32)

    near_sum[...] = jnp.zeros(near_sum.shape, F32)
    for block in range(own):
        near_sum[rep * own + block] = diag_ref[block]
    for near in range(near_total):
        lefts[near] = left_form(low_ref[near, 0:feat_dim, :], scale_sq)

    def run_chunks(chunks):
        ready = []
        for chunk in chunks:
            near, one, two = chunk_near[chunk], seats[2 * chunk], seats[2 * chunk + 1]
            right = jnp.concatenate([rights[one], rights[two]], axis=1)
            ready.append((near, one, two, wendland(lefts[near], right)))
        sums = []
        for near, one, two, weights in ready:
            vals = jnp.concatenate([far_vals[one], far_vals[two]], axis=1)
            near_vals = low_ref[near, feat_dim:width, :]
            sums.append((
                lax.dot_general(vals, weights, NT, preferred_element_type=F32),
                jnp.dot(near_vals, weights, preferred_element_type=F32),
            ))
        for (near, one, two, _), (toward_near, toward_far) in zip(ready, sums):
            near_sum[near] += toward_near
            far_sum[one] += toward_far[:, :cols]
            far_sum[two] += toward_far[:, cols:]

    @pl.loop(0, (total + UNROLL - 1) // UNROLL)
    def _(step):
        run_chunks([UNROLL * step + inner for inner in range(UNROLL)])

    for near in range(near_total):
        sums = near_sum[near]
        for target in range(reps):
            near_out[target, near * share : (near + 1) * share, :] = sums[
                target * share : (target + 1) * share
            ].astype(LINK)

    @pl.loop(0, far_total // half)
    def _(home):
        totals = [far_sum[home * half + block] for block in range(half)]
        for target in range(reps):
            far_out[target, home] = jnp.concatenate(
                [total[target * share : (target + 1) * share] for total in totals], axis=0
            ).astype(LINK)


def place_kernel(
    sites, reps, near_ref, diag_ref, far_ref, order_ref, out_ref,
    near_got, diag_got, far_got, spots, near_send, near_recv, far_send, far_recv,
):
    site, rep = lax.axis_index("site"), lax.axis_index("rep")
    total_devices = sites * reps
    me = site * reps + rep
    site_len = order_ref.shape[1]
    high_total = site_len // LOW
    share = out_ref.shape[0] // high_total
    half = near_ref.shape[1] // share
    own = diag_ref.shape[1] // share
    cols = far_ref.shape[3]

    def peer(step):
        other = lax.rem(me + step, total_devices)
        return other // reps, lax.rem(other, reps)

    barrier = pltpu.get_barrier_semaphore()

    @pl.loop(1, total_devices)
    def _(step):
        to_site, to_rep = peer(step)
        pl.semaphore_signal(barrier, inc=1, device_id={"site": to_site, "rep": to_rep})

    near_got[rep] = near_ref[rep]
    diag_got[rep] = diag_ref[rep]
    far_got[site, rep] = far_ref[rep, site]
    pl.semaphore_wait(barrier, total_devices - 1)

    def far_copy(step):
        to_site, to_rep = peer(step)
        return pltpu.make_async_remote_copy(
            src_ref=far_ref.at[to_rep, to_site], dst_ref=far_got.at[site, rep],
            send_sem=far_send.at[step], recv_sem=far_recv.at[step],
            device_id={"site": to_site, "rep": to_rep},
        )

    def rep_copies(step):
        to_rep = rep_peer(step, reps)
        copies = []
        for kind, (src, dst) in enumerate(((near_ref, near_got), (diag_ref, diag_got))):
            copies.append(pltpu.make_async_remote_copy(
                src_ref=src.at[to_rep], dst_ref=dst.at[rep],
                send_sem=near_send.at[kind, step], recv_sem=near_recv.at[kind, step],
                device_id={"rep": to_rep},
            ))
        return copies

    @pl.loop(1, total_devices)
    def _(step):
        far_copy(step).start()

    for step in range(1, reps):
        for copy in rep_copies(step):
            copy.start()

    blocks = site_len // BLOCK_LEN
    for block in range(blocks):
        index = order_ref[:, block * BLOCK_LEN : (block + 1) * BLOCK_LEN]
        hit = lax.broadcasted_iota(jnp.int32, (LOW, BLOCK_LEN), 0) == index % LOW
        spots[block] = jnp.where(hit, 1.0, 0.0).astype(BF16)

    out_ref[...] = jnp.zeros(out_ref.shape, F32)

    def put(block, rows):
        index = order_ref[:, block * BLOCK_LEN : (block + 1) * BLOCK_LEN] // LOW
        hit = lax.broadcasted_iota(jnp.int32, (high_total, BLOCK_LEN), 0) == index
        spread = jnp.concatenate(
            [
                jnp.where(hit, jnp.broadcast_to(rows[k : k + 1], hit.shape), 0.0)
                for k in range(share)
            ],
            axis=0,
        )
        coarse = spread.astype(BF16)
        fine = (spread - coarse.astype(F32)).astype(BF16)
        both = lax.dot_general(
            jnp.concatenate([coarse, fine], axis=0), spots[block], NT, preferred_element_type=F32
        )
        out_ref[...] += both[: spread.shape[0]] + both[spread.shape[0] :]

    for step in range(1, reps):
        for copy in rep_copies(step):
            copy.wait()
    near_total = near_got[0].astype(F32)
    for source in range(1, reps):
        near_total += near_got[source].astype(F32)
    for block in range(half):
        put(block, near_total[block * share : (block + 1) * share])

    @pl.loop(1, total_devices)
    def _(step):
        far_copy(step).wait()

    parts = []
    for source in range(reps):
        def add(home, total, source=source):
            return total + far_got[home, source].astype(F32)
        parts.append(lax.fori_loop(0, sites, add, jnp.zeros((half * share, cols), F32)))
    far_total = jnp.concatenate(parts, axis=1)
    for block in range(half):
        inner = (block % own) * share
        put(
            half + block,
            far_total[block * share : (block + 1) * share]
            + diag_got[block // own, inner : inner + share, :],
        )


def tiles_call(pairs, counts, scale, low, far, diag):
    reps, _, slots = pairs.shape
    half, width, _ = low.shape
    far_total, _, cols = far.shape
    side_dim = diag.shape[1]
    share = side_dim // reps
    return pl.pallas_call(
        tile_kernel,
        out_shape=(
            jax.ShapeDtypeStruct((reps, half * share, BLOCK_LEN), LINK),
            jax.ShapeDtypeStruct((reps, far_total // half, half * share, cols), LINK),
        ),
        in_specs=[SMEM, SMEM] + [VMEM] * 4,
        out_specs=(VMEM,) * 2,
        scratch_shapes=[
            pltpu.VMEM((far_total + 1, DEPTH, cols), BF16),
            pltpu.VMEM((far_total + 1, side_dim, cols), BF16),
            pltpu.VMEM((half, BLOCK_LEN, DEPTH), BF16),
            pltpu.VMEM((half, side_dim, BLOCK_LEN), F32),
            pltpu.VMEM((far_total + 1, side_dim, cols), F32),
            pltpu.SMEM((reps * slots + UNROLL,), jnp.int32),
            pltpu.SMEM((2 * (reps * slots + UNROLL),), jnp.int32),
            pltpu.SMEM((half,), jnp.int32),
        ],
        compiler_params=pltpu.CompilerParams(vmem_limit_bytes=48 * 2**20),
        name="tiles",
    )(pairs, counts, scale, low, far, diag)


def shards(features, inverse_scale, right_sides, block_order, block_pairs, pair_count):
    sites, reps = lax.axis_size("site"), lax.axis_size("rep")
    feat_dim, site_len = features.shape
    side_dim = right_sides.shape[0]
    slots = block_pairs.shape[3]
    width = feat_dim + side_dim
    blocks = site_len // BLOCK_LEN
    half = blocks // 2
    own = half // reps
    cols = BLOCK_LEN // reps
    share = side_dim // reps
    far_total = sites * half
    limit = 48 * 2**20
    sem = pltpu.SemaphoreType.DMA

    scale = inverse_scale.reshape(1, feat_dim)
    low, far, pairs, counts, low_diag, diag_part = pl.pallas_call(
        functools.partial(collect_kernel, sites, reps),
        out_shape=(
            jax.ShapeDtypeStruct((reps, own, width, BLOCK_LEN), BF16),
            jax.ShapeDtypeStruct((sites, half, width, cols), BF16),
            jax.ShapeDtypeStruct((reps, 2, slots), jnp.int32),
            jax.ShapeDtypeStruct((reps, 1, 1), jnp.int32),
            jax.ShapeDtypeStruct((own, side_dim, BLOCK_LEN), F32),
            jax.ShapeDtypeStruct((reps, own * share, BLOCK_LEN), F32),
        ),
        in_specs=[VMEM] + [HBM] * 5,
        out_specs=(VMEM,) * 6,
        scratch_shapes=[
            pltpu.VMEM(features.shape, BF16),
            pltpu.VMEM(right_sides.shape, BF16),
            pltpu.VMEM(block_order.shape, jnp.int32),
            pltpu.VMEM((site_len // LOW * width, LOW), BF16),
            pltpu.VMEM((own, width, BLOCK_LEN), BF16),
            sem((5,)), sem((3, reps)), sem((3, reps)), sem((sites,)), sem((sites,)),
        ],
        compiler_params=pltpu.CompilerParams(
            collective_id=0, has_side_effects=True, vmem_limit_bytes=limit
        ),
        name="collect",
    )(scale, features, right_sides, block_order, block_pairs, pair_count)

    near_part, far_part = tiles_call(
        pairs,
        counts,
        scale,
        low.reshape(half, width, BLOCK_LEN),
        far.reshape(far_total, width, cols),
        low_diag,
    )

    placed = pl.pallas_call(
        functools.partial(place_kernel, sites, reps),
        out_shape=jax.ShapeDtypeStruct((share * (site_len // LOW), LOW), F32),
        in_specs=[VMEM] * 4,
        out_specs=VMEM,
        scratch_shapes=[
            pltpu.VMEM((reps, half * share, BLOCK_LEN), LINK),
            pltpu.VMEM((reps, own * share, BLOCK_LEN), F32),
            pltpu.VMEM((sites, reps, half * share, cols), LINK),
            pltpu.VMEM((blocks, LOW, BLOCK_LEN), BF16),
            sem((2, reps)), sem((2, reps)), sem((sites * reps,)), sem((sites * reps,)),
        ],
        compiler_params=pltpu.CompilerParams(
            collective_id=1, has_side_effects=True, vmem_limit_bytes=limit
        ),
        name="place",
    )(near_part, diag_part, far_part, block_order)
    return placed.reshape(share, site_len)


def solution(mesh):
    placed = (
        P(None, ("groups", "site")),
        P("groups"),
        P(None, ("groups", "site")),
        P(("groups", "site"), None),
        P(("groups", "site"), "rep", None, None),
        P(("groups", "site"), "rep"),
    )
    return jax.shard_map(
        shards, mesh=mesh, in_specs=placed, out_specs=P("rep", ("groups", "site")), check_vma=False
    )
```
